128 devices in a mesh: gr: 8 (over y_hi, z), gc: 16 (over y_lo, x, core).
Axes of the slice: x: 4, y: 4 (y_hi: 2, y_lo: 2; y = y_hi * 2 + y_lo), z: 4, core: 2. Of those that a mesh axis runs over, the one named last changes fastest.
Arguments:
- student: bfloat16 [16384, 1024], P(('gr', 'gc')), may hold values from -500 to 500
- teacher: bfloat16 [16384, 1024], P(('gr', 'gc')), may hold values from -500 to 500
Outputs:
- student_grad: float32 [16384, 1024], P(('gr', 'gc'))
The draws below stay inside these ranges and needn't reach their ends.
All inputs are finite; a program needn't handle non-finite values.
Results may differ from the reference program's by a relative error of at most 0.0085.
Values may be sent and summed in bfloat16 or wider, within the bound.
A program may use at most 64 MiB of HBM per device.

```python
import math
import jax
import jax.numpy as jnp
from jax import lax

D = 1024
ROWS = 16384
N_GR = 8


def embed_draw(key, salt):
    key = jax.random.fold_in(key, salt)
    key_base, key_rows, key_cols = jax.random.split(key, 3)
    base = jnp.clip(jax.random.normal(key_base, (ROWS, D), jnp.float32), -4.0, 4.0)
    row_scale = jnp.exp(jax.random.uniform(key_rows, (ROWS, 1), jnp.float32, 0.0, math.log(10.0)))
    col_scale = jnp.exp(jax.random.uniform(key_cols, (1, D), jnp.float32, 0.0, math.log(10.0)))
    return (base * row_scale * col_scale).astype(jnp.bfloat16)


def draw_student(key, part):
    return embed_draw(key, 11)


def draw_teacher(key, part):
    return embed_draw(key, 29)


def setup_inputs(seed: int = 0) -> dict:
    key_of = jax.random.split(jax.random.key(seed), 3)
    return {
        "student": draw_student(jax.random.fold_in(key_of[2], 71), 0),
        "teacher": draw_teacher(jax.random.fold_in(key_of[2], 71), 0),
    }


def unit_rows(embedded):
    values = embedded.astype(jnp.float32)
    inverse_rms = lax.rsqrt(lax.optimization_barrier(jnp.mean(values * values, axis=-1, keepdims=True)) + 1e-06)
    unit = (values * inverse_rms * D ** (-0.5)).astype(jnp.bfloat16)
    return (unit, inverse_rms)

def reference(student, teacher):
    unit_s, inv_s = unit_rows(student)
    unit_t, inv_t = unit_rows(teacher)
    block_s = unit_s.reshape(N_GR, ROWS // N_GR, D)
    block_t = unit_t.reshape(N_GR, ROWS // N_GR, D)
    stretch = 0.5 * D ** 0.5

    def one_block(blocks):
        rows_s, rows_t = blocks
        sim_student = lax.dot_general(rows_s, unit_s, (((1,), (1,)), ((), ())), preferred_element_type=jnp.float32)
        sim_teacher = lax.dot_general(rows_t, unit_t, (((1,), (1,)), ((), ())), preferred_element_type=jnp.float32)
        mismatch = jnp.tanh(stretch * (sim_student - sim_teacher)).astype(jnp.bfloat16)
        return jnp.dot(mismatch, unit_s, preferred_element_type=jnp.float32)
    pull = lax.map(one_block, (block_s, block_t)).reshape(ROWS, D)
    unit_float = unit_s.astype(jnp.float32)
    radial = lax.optimization_barrier(jnp.sum(unit_float * pull, axis=-1, keepdims=True))
    factor = 12.0 * (D / ROWS) ** 0.5
    return factor * inv_s * (pull - radial * unit_float)
```

```python
import jax
import jax.numpy as jnp
from jax import lax
from jax.experimental import pallas as pl
from jax.experimental.pallas import tpu as pltpu
from jax.sharding import PartitionSpec as P

D = 1024
F32 = jnp.float32
BF16 = jnp.bfloat16
MESH = pl.DeviceIdType.MESH

HELD = (30, 0, 48, 100, 32, 124, 93, 29, 22, 84, 21, 85, 4, 26, 20, 94)
PARENT = ((13, 2, 4, 14, 3, 2, 7, 15, 10, 11, 11, -1, 14, 8, 9, 0), (13, 2, 4, 9, 3, 2, 7, 0, 11, 11, 11, -1, 9, 8, 9, 0), (13, 12, 1, 14, 2, 2, 7, 0, 10, 10, 11, -1, 14, 8, 9, 0), (13, 12, 1, 9, 2, 2, 0, 6, 10, 11, 11, -1, 9, 8, 9, 0))
SLOT = ((6, 7, 5, 3, 4, 9, 7, 7, 1, 2, -1, -1, 5, 5, 2, 6), (8, 8, 4, 2, 3, 8, 9, 9, 3, 1, -1, -1, 2, 7, 1, 8), (2, 5, 6, 6, 8, 7, 4, 4, 0, 3, -1, -1, 4, 1, 3, 2), (4, 2, 3, 1, 7, 6, 5, 5, 2, 0, -1, -1, 1, 3, 0, 4))
TASKS = ((4, 4), (5, 1), (4, 1), (6, 5), (6, 4), (6, 1), (7, 6), (7, 4), (5, 0), (4, 0), (7, 2), (6, 3), (6, 2), (5, 2), (4, 2), (3, 2), (3, 1), (3, 0), (2, 1), (2, 0))
N = len(HELD)
ROWS = 128
PIECES = len(PARENT)
PIECE = ROWS // PIECES
OWN = PARENT[0].index(-1)
STAGES = 1 + max(map(max, SLOT))
PER_STAGE = 3


def parts(offset):
    return tuple((offset >> s) & 3 for s in (0, 2, 4)) + (offset >> 6,)


def minus(a, b):
    sizes = (4, 4, 4, 2)
    return tuple((p - q) % n for p, q, n in zip(parts(a), parts(b), sizes))


def same_chip(h, j):
    return minus(HELD[PARENT[h][j]], HELD[j])[:3] == (0, 0, 0)


def stages():
    out = [[] for _ in range(STAGES + 1)]
    for h in range(PIECES):
        for j in range(N):
            if j != OWN:
                near = same_chip(h, j)
                out[SLOT[h][j] + near].append((h, j, PARENT[h][j], near))
    for t, sends in enumerate(out):
        fresh = {(h, j) for h, j, _, near in sends if near}
        sends.sort(key=lambda s: (not s[3], (s[0], s[2]) in fresh))
    return [[s[:3] for s in sends] for sends in out]


def weights():
    done, out = set(), []
    for g, h in TASKS:
        quad = [[0.0, 0.0], [0.0, 0.0]]
        for p in range(2):
            for q in range(2):
                a, b = HELD[2 * g + p], HELD[2 * h + q]
                there, back = minus(a, b), minus(b, a)
                if min(there, back) in done:
                    continue
                if g == h and p < q:
                    continue
                done.add(min(there, back))
                weight = 0.5 if there == back and any(there) else 1.0
                quad[p][q] = weight
                if g == h:
                    quad[q][p] = weight
        out.append(quad)
    assert len(done) == 72
    return out


def kernel(student_ref, teacher_ref, out_ref, held, pull, sent, come, g_send, g_recv, r_send, r_recv):
    gr, gc = lax.axis_index("gr"), lax.axis_index("gc")
    place = (lax.rem(gc // 2, 4), (gr // 4) * 2 + gc // 8, lax.rem(gr, 4), lax.rem(gc, 2))

    def device(step):
        x, y, z, c = (lax.rem(p + s, n) for p, s, n in zip(place, step, (4, 4, 4, 2)))
        return ((y // 2) * 4 + z, lax.rem(y, 2) * 8 + x * 2 + c)

    plan = stages()
    edges = [e for sends in plan for e in sends]
    steps = set()
    for h, j, i in edges:
        steps |= {minus(HELD[i], HELD[j]), minus(HELD[j], HELD[i])}
    target = {step: device(step) for step in sorted(steps)}

    barrier = pltpu.get_barrier_semaphore()
    for step in target:
        pl.semaphore_signal(barrier, inc=1, device_id=target[step], device_id_type=MESH)

    def unit(ref, rows):
        values = ref[rows, :].astype(F32)
        inverse = lax.rsqrt(jnp.mean(values * values, axis=-1, keepdims=True) + 1e-06)
        return (values * inverse * D ** (-0.5)).astype(BF16), inverse

    def rows_of(h):
        return pl.ds(h * PIECE, PIECE)

    for h in range(PIECES):
        held[OWN, rows_of(h), 0:D] = unit(student_ref, rows_of(h))[0]
        held[OWN, rows_of(h), D : 2 * D] = unit(teacher_ref, rows_of(h))[0]
    pl.semaphore_wait(barrier, len(target))

    arrived = {(h, OWN) for h in range(PIECES)}
    gathers, returns = {}, {}

    def await_piece(h, j):
        if (h, j) not in arrived:
            gathers[h, j].wait_recv()
            arrived.add((h, j))

    tasks = list(zip(TASKS, weights()))
    fresh = set(range(N // 2))

    def add(g, value):
        value = value.reshape(2, ROWS, D)
        if g in fresh:
            pull[2 * g : 2 * g + 2] = value
            fresh.discard(g)
        else:
            pull[2 * g : 2 * g + 2] += value

    def dot(a, b, dims):
        return lax.dot_general(a, b, (dims, ((), ())), preferred_element_type=F32)

    def run(task):
        (g, h), quad = task
        for b in (2 * g, 2 * g + 1, 2 * h, 2 * h + 1):
            for piece in range(PIECES):
                await_piece(piece, b)
        s_g = held[2 * g : 2 * g + 2, :, 0:D].reshape(2 * ROWS, D)
        s_h = held[2 * h : 2 * h + 2, :, 0:D].reshape(2 * ROWS, D)
        t_g = held[2 * g : 2 * g + 2, :, D : 2 * D].reshape(2 * ROWS, D)
        t_h = held[2 * h : 2 * h + 2, :, D : 2 * D].reshape(2 * ROWS, D)
        gap = dot(s_g, s_h, ((1,), (1,))) - dot(t_g, t_h, ((1,), (1,)))
        lines = []
        for p in range(2):
            line = []
            for q in range(2):
                if quad[p][q] == 0.0:
                    line.append(jnp.zeros((ROWS, ROWS), BF16))
                    continue
                part = gap[p * ROWS : (p + 1) * ROWS, q * ROWS : (q + 1) * ROWS]
                value = jnp.tanh(0.5 * D**0.5 * part).astype(BF16)
                line.append(value if quad[p][q] == 1.0 else value * jnp.asarray(quad[p][q], BF16))
            lines.append(jnp.concatenate(line, axis=1))
        mismatch = jnp.concatenate(lines, axis=0)
        add(g, dot(mismatch, s_h, ((1,), (0,))))
        if g != h:
            add(h, dot(mismatch, s_g, ((0,), (0,))))


    ready = [0] * (N // 2)
    for h, j, _ in edges:
        ready[j // 2] = max(ready[j // 2], SLOT[h][j] + 1 + same_chip(h, j))

    for t, sends in enumerate(plan):
        for h, j, i in sends:
            await_piece(h, i)
            gathers[h, j] = pltpu.make_async_remote_copy(
                src_ref=held.at[i, rows_of(h), :],
                dst_ref=held.at[j, rows_of(h), :],
                send_sem=g_send.at[h, j],
                recv_sem=g_recv.at[h, j],
                device_id=target[minus(HELD[i], HELD[j])],
                device_id_type=MESH,
            )
            gathers[h, j].start()
        for task in [k for k in tasks if max(ready[b] for b in k[0]) <= t][:PER_STAGE]:
            run(task)
            tasks.remove(task)

    def total(h, j):
        for task in [k for k in tasks if j // 2 in k[0]]:
            run(task)
            tasks.remove(task)
        value = pull[j, rows_of(h), :]
        for child in range(N):
            if PARENT[h][child] == j:
                returns[h, child].wait_recv()
                value += come[child, rows_of(h), :].astype(F32)
        return value

    for h, j, i in reversed(edges):
        sent[j, rows_of(h), :] = total(h, j).astype(BF16)
        returns[h, j] = pltpu.make_async_remote_copy(
            src_ref=sent.at[j, rows_of(h), :],
            dst_ref=come.at[j, rows_of(h), :],
            send_sem=r_send.at[h, j],
            recv_sem=r_recv.at[h, j],
            device_id=target[minus(HELD[j], HELD[i])],
            device_id_type=MESH,
        )
        returns[h, j].start()

    scale = 12.0 * (D / (ROWS * 128)) ** 0.5
    for h in range(PIECES):
        value = total(h, OWN)
        unit_float = held[OWN, rows_of(h), 0:D].astype(F32)
        inverse = unit(student_ref, rows_of(h))[1]
        radial = jnp.sum(unit_float * value, axis=-1, keepdims=True)
        out_ref[rows_of(h), :] = scale * inverse * (value - radial * unit_float)
    for h, j, _ in edges:
        await_piece(h, j)
        gathers[h, j].wait_send()
        returns[h, j].wait_send()


def local(student, teacher):
    vmem = pl.BlockSpec(memory_space=pltpu.VMEM)
    sems = pltpu.SemaphoreType.DMA((PIECES, N))
    return pl.pallas_call(
        kernel,
        out_shape=jax.ShapeDtypeStruct((ROWS, D), F32),
        in_specs=[vmem, vmem],
        out_specs=vmem,
        scratch_shapes=[
            pltpu.VMEM((N, ROWS, 2 * D), BF16),
            pltpu.VMEM((N, ROWS, D), F32),
            pltpu.VMEM((N, ROWS, D), BF16),
            pltpu.VMEM((N, ROWS, D), BF16),
            sems,
            sems,
            sems,
            sems,
        ],
        compiler_params=pltpu.CompilerParams(
            collective_id=0, has_side_effects=True, vmem_limit_bytes=56 * 2**20
        ),
        name="relational_grad",
    )(student, teacher)


def solution(mesh):
    spec = P(("gr", "gc"), None)
    return jax.shard_map(local, mesh=mesh, in_specs=(spec, spec), out_specs=spec, check_vma=False)
```

```python
import jax
import jax.numpy as jnp
from jax import lax
from jax.experimental import pallas as pl
from jax.experimental.pallas import tpu as pltpu
from jax.sharding import PartitionSpec as P

D = 1024
F32 = jnp.float32
BF16 = jnp.bfloat16
MESH = pl.DeviceIdType.MESH

HELD = (72, 76, 91, 89, 113, 125, 49, 126, 11, 24, 124, 62, 0, 64, 59, 123)
STEPS = ((0, 6, 5), (5, 10, 5), (5, 11, 5), (2, 7, 5), (6, 10, 5), (7, 6, 5), (1, 10, 5), (2, 4, 5), (6, 11, 5), (1, 11, 5), (5, 6, 5), (7, 10, 5), (0, 4, 6), (5, 1, 10), (5, 7, 11), (3, 4, 5), (3, 7, 5), (4, 10, 5), (2, 11, 7), (6, 1, 10), (7, 4, 6), (1, 4, 5), (3, 10, 5), (7, 11, 5), (1, 1, 10), (2, 6, 4), (6, 7, 11), (5, 0, 1), (0, 10, 5), (0, 11, 5), (6, 4, 5), (1, 7, 11), (5, 4, 6), (7, 1, 10), (6, 0, 1), (2, 10, 5), (4, 7, 5), (5, 12, 1), (3, 6, 4), (3, 11, 7), (4, 1, 10), (1, 0, 1), (5, 9, 0), (1, 6, 4), (7, 7, 11), (3, 1, 10), (7, 0, 1), (7, 12, 1), (6, 8, 0), (6, 12, 1), (0, 7, 11), (6, 6, 4), (4, 0, 1), (1, 8, 0), (4, 4, 5), (2, 1, 10), (4, 11, 7), (5, 13, 12), (1, 9, 0), (5, 3, 9), (5, 2, 9), (5, 5), (7, 13, 12), (7, 8, 0), (6, 14, 8), (0, 1, 10), (3, 0, 1), (3, 13, 1), (6, 13, 12), (4, 8, 0), (1, 15, 8), (6, 9, 0), (2, 0, 1), (2, 12, 1), (1, 12, 1), (4, 6, 4), (5, 8, 2), (4, 9, 0), (1, 3, 9), (6, 15, 14), (3, 8, 0), (4, 12, 1), (3, 12, 13), (7, 14, 8), (0, 0, 1), (1, 14, 15), (2, 8, 0), (2, 9, 0), (0, 12, 1), (2, 13, 12), (1, 2, 9), (4, 15, 8), (3, 9, 0), (6, 3, 9), (5, 2), (1, 13, 12), (3, 14, 8), (7, 9, 0), (4, 3, 9), (7, 15, 14), (0, 8, 0), (4, 13, 12), (4, 2, 9), (2, 14, 8), (0, 9, 0), (2, 3, 9), (5, 15, 8), (4, 14, 15), (5, 3), (0, 13, 12), (2, 2, 9), (6, 2, 8), (3, 3, 9), (3, 15, 14), (5, 0), (3, 2, 9), (0, 15, 8), (0, 2, 8), (7, 3, 9), (2, 15, 14), (3, 0), (7, 2, 9), (0, 3, 9), (5, 14, 15), (2, 0), (6, 5), (0, 14, 15))
LATE = ((6, 2), (6, 0), (6, 4), (5, 4), (4, 3), (4, 2), (4, 0), (7, 6), (7, 4), (7, 2), (7, 0), (7, 1), (5, 1), (3, 1), (2, 1))
RETURNS = ((2, 14, 15), (2, 2, 8), (2, 3, 9), (2, 15, 8), (3, 14, 15), (3, 2, 9), (3, 3, 9), (3, 15, 8), (1, 14, 15), (0, 2, 8), (1, 2, 9), (1, 3, 9), (1, 15, 8), (0, 14, 15), (2, 8, 0), (2, 9, 0), (0, 3, 9), (0, 15, 8), (3, 8, 0), (3, 9, 0), (1, 8, 0), (1, 9, 0), (2, 13, 12), (2, 0, 1), (2, 12, 1), (0, 8, 0), (0, 9, 0), (3, 12, 13), (3, 0, 1), (3, 13, 1), (1, 13, 12), (1, 0, 1), (1, 12, 1), (0, 13, 12), (2, 1, 10), (0, 0, 1), (0, 12, 1), (3, 1, 10), (1, 1, 10), (0, 4, 6), (2, 11, 7), (0, 6, 5), (2, 7, 5), (2, 10, 5), (0, 1, 10), (1, 7, 11), (3, 6, 4), (1, 11, 5), (3, 4, 5), (3, 10, 5), (0, 11, 7), (1, 4, 6), (0, 7, 5), (1, 6, 5), (1, 10, 5), (2, 4, 6), (3, 11, 7), (0, 10, 5), (2, 6, 5), (3, 7, 5))
N = len(HELD)
ROWS = 128
TASKS = tuple(s for s in STEPS if len(s) == 2) + LATE
SENDS = tuple(s for s in STEPS if len(s) == 3)
OWN = ({i for _, _, i in SENDS} - {j for _, j, _ in SENDS}).pop()
PIECES = 1 + max(h for h, _, _ in SENDS)
PARTS = 1 + max(h for h, _, _ in RETURNS)


def parts(offset):
    return tuple((offset >> s) & 3 for s in (0, 2, 4)) + (offset >> 6,)


def minus(a, b):
    sizes = (4, 4, 4, 2)
    return tuple((p - q) % n for p, q, n in zip(parts(a), parts(b), sizes))


def weights():
    done, out = set(), []
    for g, h in TASKS:
        quad = [[0.0, 0.0], [0.0, 0.0]]
        for p in range(2):
            for q in range(2):
                a, b = HELD[2 * g + p], HELD[2 * h + q]
                there, back = minus(a, b), minus(b, a)
                if min(there, back) in done:
                    continue
                if g == h and p < q:
                    continue
                done.add(min(there, back))
                weight = 0.5 if there == back and any(there) else 1.0
                quad[p][q] = weight
                if g == h:
                    quad[q][p] = weight
        out.append(quad)
    assert len(done) == 72
    return out


def kernel(student_ref, teacher_ref, out_ref, held, pull, sent, come, g_send, g_recv, r_send, r_recv):
    gr, gc = lax.axis_index("gr"), lax.axis_index("gc")
    place = (lax.rem(gc // 2, 4), (gr // 4) * 2 + gc // 8, lax.rem(gr, 4), lax.rem(gc, 2))

    def device(step):
        x, y, z, c = (lax.rem(p + s, n) for p, s, n in zip(place, step, (4, 4, 4, 2)))
        return ((y // 2) * 4 + z, lax.rem(y, 2) * 8 + x * 2 + c)

    steps = set()
    for _, j, i in SENDS + RETURNS:
        steps |= {minus(HELD[i], HELD[j]), minus(HELD[j], HELD[i])}
    target = {step: device(step) for step in sorted(steps)}

    barrier = pltpu.get_barrier_semaphore()
    for step in target:
        pl.semaphore_signal(barrier, inc=1, device_id=target[step], device_id_type=MESH)

    def unit(ref, rows):
        values = ref[rows, :].astype(F32)
        inverse = lax.rsqrt(jnp.mean(values * values, axis=-1, keepdims=True) + 1e-06)
        return (values * inverse * D ** (-0.5)).astype(BF16), inverse

    def rows_of(h):
        return pl.ds(h * (ROWS // PIECES), ROWS // PIECES)

    def part_of(h):
        return pl.ds(h * (ROWS // PARTS), ROWS // PARTS)

    for h in range(PIECES):
        held[OWN, rows_of(h), 0:D] = unit(student_ref, rows_of(h))[0]
        held[OWN, rows_of(h), D : 2 * D] = unit(teacher_ref, rows_of(h))[0]
    pl.semaphore_wait(barrier, len(target))

    arrived = {(h, OWN) for h in range(PIECES)}
    gathers, returns = {}, {}

    def await_piece(h, j):
        if (h, j) not in arrived:
            gathers[h, j].wait_recv()
            arrived.add((h, j))

    tasks = list(zip(TASKS, weights()))
    fresh = set(range(N // 2))

    def add(g, value):
        value = value.reshape(2, ROWS, D)
        if g in fresh:
            pull[2 * g : 2 * g + 2] = value
            fresh.discard(g)
        else:
            pull[2 * g : 2 * g + 2] += value

    def dot(a, b, dims):
        return lax.dot_general(a, b, (dims, ((), ())), preferred_element_type=F32)

    def run(task):
        (g, h), quad = task
        for b in (2 * g, 2 * g + 1, 2 * h, 2 * h + 1):
            for piece in range(PIECES):
                await_piece(piece, b)
        s_g = held[2 * g : 2 * g + 2, :, 0:D].reshape(2 * ROWS, D)
        s_h = held[2 * h : 2 * h + 2, :, 0:D].reshape(2 * ROWS, D)
        t_g = held[2 * g : 2 * g + 2, :, D : 2 * D].reshape(2 * ROWS, D)
        t_h = held[2 * h : 2 * h + 2, :, D : 2 * D].reshape(2 * ROWS, D)
        gap = dot(s_g, s_h, ((1,), (1,))) - dot(t_g, t_h, ((1,), (1,)))
        lines = []
        for p in range(2):
            line = []
            for q in range(2):
                if quad[p][q] == 0.0:
                    line.append(jnp.zeros((ROWS, ROWS), BF16))
                    continue
                part = gap[p * ROWS : (p + 1) * ROWS, q * ROWS : (q + 1) * ROWS]
                value = jnp.tanh(0.5 * D**0.5 * part).astype(BF16)
                line.append(value if quad[p][q] == 1.0 else value * jnp.asarray(quad[p][q], BF16))
            lines.append(jnp.concatenate(line, axis=1))
        mismatch = jnp.concatenate(lines, axis=0)
        add(g, dot(mismatch, s_h, ((1,), (0,))))
        if g != h:
            add(h, dot(mismatch, s_g, ((0,), (0,))))

    for step in STEPS:
        if len(step) == 2:
            run(tasks.pop(0))
            continue
        h, j, i = step
        await_piece(h, i)
        gathers[h, j] = pltpu.make_async_remote_copy(
            src_ref=held.at[i, rows_of(h), :],
            dst_ref=held.at[j, rows_of(h), :],
            send_sem=g_send.at[h, j],
            recv_sem=g_recv.at[h, j],
            device_id=target[minus(HELD[i], HELD[j])],
            device_id_type=MESH,
        )
        gathers[h, j].start()

    def total(h, j):
        for task in [k for k in tasks if j // 2 in k[0]]:
            run(task)
            tasks.remove(task)
        value = pull[j, part_of(h), :]
        for part, child, parent in RETURNS:
            if (part, parent) == (h, j):
                returns[h, child].wait_recv()
                value += come[child, part_of(h), :].astype(F32)
        return value

    for h, j, i in RETURNS:
        sent[j, part_of(h), :] = total(h, j).astype(BF16)
        returns[h, j] = pltpu.make_async_remote_copy(
            src_ref=sent.at[j, part_of(h), :],
            dst_ref=come.at[j, part_of(h), :],
            send_sem=r_send.at[h, j],
            recv_sem=r_recv.at[h, j],
            device_id=target[minus(HELD[j], HELD[i])],
            device_id_type=MESH,
        )
        returns[h, j].start()

    scale = 12.0 * (D / (ROWS * 128)) ** 0.5
    for h in range(PARTS):
        value = total(h, OWN)
        unit_float = held[OWN, part_of(h), 0:D].astype(F32)
        inverse = unit(student_ref, part_of(h))[1]
        radial = jnp.sum(unit_float * value, axis=-1, keepdims=True)
        out_ref[part_of(h), :] = scale * inverse * (value - radial * unit_float)
    for h, j, _ in SENDS:
        gathers[h, j].wait_send()
    for h, j, _ in RETURNS:
        returns[h, j].wait_send()


def local(student, teacher):
    vmem = pl.BlockSpec(memory_space=pltpu.VMEM)
    g_sems = pltpu.SemaphoreType.DMA((PIECES, N))
    r_sems = pltpu.SemaphoreType.DMA((PARTS, N))
    return pl.pallas_call(
        kernel,
        out_shape=jax.ShapeDtypeStruct((ROWS, D), F32),
        in_specs=[vmem, vmem],
        out_specs=vmem,
        scratch_shapes=[
            pltpu.VMEM((N, ROWS, 2 * D), BF16),
            pltpu.VMEM((N, ROWS, D), F32),
            pltpu.VMEM((N, ROWS, D), BF16),
            pltpu.VMEM((N, ROWS, D), BF16),
            g_sems,
            g_sems,
            r_sems,
            r_sems,
        ],
        compiler_params=pltpu.CompilerParams(
            collective_id=0, has_side_effects=True, vmem_limit_bytes=56 * 2**20
        ),
        name="relational_grad",
    )(student, teacher)


def solution(mesh):
    spec = P(("gr", "gc"), None)
    return jax.shard_map(local, mesh=mesh, in_specs=(spec, spec), out_specs=spec, check_vma=False)
```

```python
import jax
import jax.numpy as jnp
from jax import lax
from jax.experimental import pallas as pl
from jax.experimental.pallas import tpu as pltpu
from jax.sharding import PartitionSpec as P

D = 1024
F32 = jnp.float32
BF16 = jnp.bfloat16
MESH = pl.DeviceIdType.MESH

HELD = (35, 33, 73, 9, 69, 5, 80, 48, 3, 65, 64, 32, 13, 77, 113, 19)
STEPS = ((2, 6, 10), (2, 8, 10), (4, 9, 10), (6, 7, 10), (1, 7, 10), (1, 8, 10), (7, 6, 10), (7, 9, 10), (2, 9, 10), (3, 6, 10), (3, 7, 10), (3, 8, 10), (6, 9, 10), (7, 8, 10), (4, 5, 9), (4, 12, 9), (2, 11, 6), (6, 11, 7), (1, 9, 10), (6, 8, 10), (7, 5, 9), (7, 12, 9), (1, 11, 7), (7, 11, 6), (0, 9, 10), (4, 6, 10), (5, 8, 10), (7, 14, 9), (2, 4, 9), (2, 12, 9), (4, 4, 5), (4, 13, 12), (1, 15, 8), (3, 9, 10), (4, 8, 10), (5, 7, 10), (6, 4, 9), (6, 13, 9), (7, 4, 5), (7, 13, 12), (0, 8, 10), (2, 14, 9), (3, 11, 6), (5, 9, 10), (1, 4, 9), (1, 12, 9), (2, 5, 4), (2, 13, 12), (0, 7, 10), (1, 14, 7), (0, 5, 9), (0, 13, 9), (4, 11, 6), (4, 15, 6), (6, 5, 4), (6, 12, 13), (5, 15, 8), (6, 1, 11), (7, 0, 11), (3, 5, 9), (3, 12, 9), (5, 11, 7), (1, 5, 4), (1, 13, 12), (3, 14, 7), (4, 14, 9), (6, 15, 8), (5, 5, 9), (5, 12, 9), (3, 0, 11), (1, 2, 12), (2, 3, 5), (0, 4, 5), (0, 12, 13), (4, 4), (0, 15, 8), (2, 15, 6), (0, 11, 7), (0, 14, 7), (4, 2, 13), (7, 3, 4), (3, 4, 5), (3, 13, 12), (1, 0, 15), (1, 1, 14), (3, 15, 6), (5, 14, 7), (0, 2, 13), (3, 2, 4), (5, 4, 5), (5, 13, 12), (2, 1, 14), (4, 0, 11), (6, 14, 7), (7, 15, 8), (5, 3, 13), (6, 3, 4), (1, 3, 2), (2, 2, 3), (6, 6), (1, 6, 15), (6, 6, 11), (7, 7, 11), (0, 0, 11), (4, 3, 2), (7, 2, 3), (6, 4), (2, 7, 14), (3, 1, 14), (5, 0, 15), (5, 1, 11), (0, 3, 2), (3, 3, 2), (6, 5), (0, 1, 11), (2, 0, 15), (4, 7, 14), (5, 6, 11), (5, 2, 3), (6, 2, 3), (5, 4), (0, 6, 10), (4, 1, 14), (6, 0, 11), (7, 1, 11))
LATE = ((5, 2), (7, 6), (7, 5), (7, 2), (7, 1), (5, 1), (4, 1), (7, 0), (6, 3), (6, 0), (4, 0), (3, 2), (3, 1), (1, 0), (0, 0))
RETURNS = ((1, 2, 3), (0, 14, 1), (1, 3, 5), (3, 2, 3), (1, 0, 11), (1, 1, 11), (3, 1, 14), (3, 3, 12), (0, 2, 3), (2, 3, 2), (1, 15, 6), (2, 1, 11), (2, 7, 10), (3, 0, 15), (0, 3, 5), (2, 2, 13), (1, 4, 5), (1, 12, 13), (0, 0, 11), (0, 1, 11), (2, 0, 15), (2, 14, 9), (1, 5, 9), (1, 13, 9), (3, 5, 4), (3, 13, 12), (0, 15, 8), (1, 8, 10), (1, 11, 7), (1, 14, 7), (3, 4, 9), (3, 12, 9), (0, 4, 5), (0, 12, 13), (0, 6, 10), (3, 11, 7), (3, 14, 7), (3, 15, 6), (0, 5, 9), (0, 13, 9), (2, 5, 4), (2, 13, 12), (0, 11, 7), (1, 9, 10), (2, 11, 6), (2, 15, 6), (2, 4, 9), (2, 12, 9), (1, 6, 10), (1, 7, 10), (2, 8, 10), (3, 9, 10), (0, 9, 10), (3, 6, 10), (3, 7, 10), (3, 8, 10), (0, 7, 10), (0, 8, 10), (2, 6, 10), (2, 9, 10))
N = len(HELD)
ROWS = 128
TASKS = tuple(s for s in STEPS if len(s) == 2) + LATE
SENDS = tuple(s for s in STEPS if len(s) == 3)
OWN = ({i for _, _, i in SENDS} - {j for _, j, _ in SENDS}).pop()
PIECES = 1 + max(h for h, _, _ in SENDS)
PARTS = 1 + max(h for h, _, _ in RETURNS)


def parts(offset):
    return tuple((offset >> s) & 3 for s in (0, 2, 4)) + (offset >> 6,)


def minus(a, b):
    sizes = (4, 4, 4, 2)
    return tuple((p - q) % n for p, q, n in zip(parts(a), parts(b), sizes))


def weights():
    done, out = set(), []
    for g, h in TASKS:
        quad = [[0.0, 0.0], [0.0, 0.0]]
        for p in range(2):
            for q in range(2):
                a, b = HELD[2 * g + p], HELD[2 * h + q]
                there, back = minus(a, b), minus(b, a)
                if min(there, back) in done:
                    continue
                if g == h and p < q:
                    continue
                done.add(min(there, back))
                weight = 0.5 if there == back and any(there) else 1.0
                quad[p][q] = weight
                if g == h:
                    quad[q][p] = weight
        out.append(quad)
    assert len(done) == 72
    return out


def kernel(student_ref, teacher_ref, out_ref, held, pull, sent, come, g_send, g_recv, r_send, r_recv):
    gr, gc = lax.axis_index("gr"), lax.axis_index("gc")
    place = (lax.rem(gc // 2, 4), (gr // 4) * 2 + gc // 8, lax.rem(gr, 4), lax.rem(gc, 2))

    def device(step):
        x, y, z, c = (lax.rem(p + s, n) for p, s, n in zip(place, step, (4, 4, 4, 2)))
        return ((y // 2) * 4 + z, lax.rem(y, 2) * 8 + x * 2 + c)

    steps = set()
    for _, j, i in SENDS + RETURNS:
        steps |= {minus(HELD[i], HELD[j]), minus(HELD[j], HELD[i])}
    target = {step: device(step) for step in sorted(steps)}

    barrier = pltpu.get_barrier_semaphore()
    for step in target:
        pl.semaphore_signal(barrier, inc=1, device_id=target[step], device_id_type=MESH)

    def unit(ref, rows):
        values = ref[rows, :].astype(F32)
        inverse = lax.rsqrt(jnp.mean(values * values, axis=-1, keepdims=True) + 1e-06)
        return (values * inverse * D ** (-0.5)).astype(BF16), inverse

    def rows_of(h):
        return pl.ds(h * (ROWS // PIECES), ROWS // PIECES)

    def part_of(h):
        return pl.ds(h * (ROWS // PARTS), ROWS // PARTS)

    for h in range(PIECES):
        held[OWN, rows_of(h), 0:D] = unit(student_ref, rows_of(h))[0]
        held[OWN, rows_of(h), D : 2 * D] = unit(teacher_ref, rows_of(h))[0]
    pl.semaphore_wait(barrier, len(target))

    arrived = {(h, OWN) for h in range(PIECES)}
    gathers, returns = {}, {}

    def await_piece(h, j):
        if (h, j) not in arrived:
            gathers[h, j].wait_recv()
            arrived.add((h, j))

    tasks = list(zip(TASKS, weights()))
    fresh = set(range(N // 2))

    def add(g, value):
        value = value.reshape(2, ROWS, D)
        if g in fresh:
            pull[2 * g : 2 * g + 2] = value
            fresh.discard(g)
        else:
            pull[2 * g : 2 * g + 2] += value

    def dot(a, b, dims):
        return lax.dot_general(a, b, (dims, ((), ())), preferred_element_type=F32)

    def run(task):
        (g, h), quad = task
        for b in (2 * g, 2 * g + 1, 2 * h, 2 * h + 1):
            for piece in range(PIECES):
                await_piece(piece, b)
        s_g = held[2 * g : 2 * g + 2, :, 0:D].reshape(2 * ROWS, D)
        s_h = held[2 * h : 2 * h + 2, :, 0:D].reshape(2 * ROWS, D)
        t_g = held[2 * g : 2 * g + 2, :, D : 2 * D].reshape(2 * ROWS, D)
        t_h = held[2 * h : 2 * h + 2, :, D : 2 * D].reshape(2 * ROWS, D)
        gap = dot(s_g, s_h, ((1,), (1,))) - dot(t_g, t_h, ((1,), (1,)))
        lines = []
        for p in range(2):
            line = []
            for q in range(2):
                if quad[p][q] == 0.0:
                    line.append(jnp.zeros((ROWS, ROWS), BF16))
                    continue
                part = gap[p * ROWS : (p + 1) * ROWS, q * ROWS : (q + 1) * ROWS]
                value = jnp.tanh(0.5 * D**0.5 * part).astype(BF16)
                line.append(value if quad[p][q] == 1.0 else value * jnp.asarray(quad[p][q], BF16))
            lines.append(jnp.concatenate(line, axis=1))
        mismatch = jnp.concatenate(lines, axis=0)
        add(g, dot(mismatch, s_h, ((1,), (0,))))
        if g != h:
            add(h, dot(mismatch, s_g, ((0,), (0,))))

    for step in STEPS:
        if len(step) == 2:
            run(tasks.pop(0))
            continue
        h, j, i = step
        await_piece(h, i)
        gathers[h, j] = pltpu.make_async_remote_copy(
            src_ref=held.at[i, rows_of(h), :],
            dst_ref=held.at[j, rows_of(h), :],
            send_sem=g_send.at[h, j],
            recv_sem=g_recv.at[h, j],
            device_id=target[minus(HELD[i], HELD[j])],
            device_id_type=MESH,
        )
        gathers[h, j].start()

    def total(h, j):
        for task in [k for k in tasks if j // 2 in k[0]]:
            run(task)
            tasks.remove(task)
        value = pull[j, part_of(h), :]
        for part, child, parent in RETURNS:
            if (part, parent) == (h, j):
                returns[h, child].wait_recv()
                value += come[child, part_of(h), :].astype(F32)
        return value

    for h, j, i in RETURNS:
        sent[j, part_of(h), :] = total(h, j).astype(BF16)
        returns[h, j] = pltpu.make_async_remote_copy(
            src_ref=sent.at[j, part_of(h), :],
            dst_ref=come.at[j, part_of(h), :],
            send_sem=r_send.at[h, j],
            recv_sem=r_recv.at[h, j],
            device_id=target[minus(HELD[j], HELD[i])],
            device_id_type=MESH,
        )
        returns[h, j].start()

    scale = 12.0 * (D / (ROWS * 128)) ** 0.5
    for h in range(PARTS):
        value = total(h, OWN)
        unit_float = held[OWN, part_of(h), 0:D].astype(F32)
        inverse = unit(student_ref, part_of(h))[1]
        radial = jnp.sum(unit_float * value, axis=-1, keepdims=True)
        out_ref[part_of(h), :] = scale * inverse * (value - radial * unit_float)
    for h, j, _ in SENDS:
        gathers[h, j].wait_send()
    for h, j, _ in RETURNS:
        returns[h, j].wait_send()


def local(student, teacher):
    vmem = pl.BlockSpec(memory_space=pltpu.VMEM)
    g_sems = pltpu.SemaphoreType.DMA((PIECES, N))
    r_sems = pltpu.SemaphoreType.DMA((PARTS, N))
    return pl.pallas_call(
        kernel,
        out_shape=jax.ShapeDtypeStruct((ROWS, D), F32),
        in_specs=[vmem, vmem],
        out_specs=vmem,
        scratch_shapes=[
            pltpu.VMEM((N, ROWS, 2 * D), BF16),
            pltpu.VMEM((N, ROWS, D), F32),
            pltpu.VMEM((N, ROWS, D), BF16),
            pltpu.VMEM((N, ROWS, D), BF16),
            g_sems,
            g_sems,
            r_sems,
            r_sems,
        ],
        compiler_params=pltpu.CompilerParams(
            collective_id=0, has_side_effects=True, vmem_limit_bytes=56 * 2**20
        ),
        name="relational_grad",
    )(student, teacher)


def solution(mesh):
    spec = P(("gr", "gc"), None)
    return jax.shard_map(local, mesh=mesh, in_specs=(spec, spec), out_specs=spec, check_vma=False)
```

```python
import jax
import jax.numpy as jnp
from jax import lax
from jax.experimental import pallas as pl
from jax.experimental.pallas import tpu as pltpu
from jax.sharding import PartitionSpec as P

D = 1024
F32 = jnp.float32
BF16 = jnp.bfloat16
MESH = pl.DeviceIdType.MESH

HELD = (112, 19, 67, 64, 69, 113, 1, 13, 5, 77, 32, 80, 9, 73, 33, 35)
STEPS = ((0, 0, 2, 3), (0, 1, 6, 3), (0, 1, 0, 3), (0, 3, 11, 3), (0, 0, 6, 3), (0, 0, 0, 3), (0, 1, 2, 3), (0, 1, 11, 3), (0, 2, 6, 3), (0, 2, 11, 3), (0, 3, 2, 3), (0, 3, 0, 3), (0, 1, 4, 6), (0, 1, 9, 6), (0, 0, 11, 3), (0, 2, 2, 3), (0, 2, 0, 3), (0, 3, 6, 3), (0, 0, 7, 6), (0, 0, 4, 6), (0, 1, 8, 4), (0, 1, 7, 9), (0, 1, 1, 11), (0, 1, 10, 0), (0, 2, 7, 6), (0, 2, 4, 6), (0, 2, 10, 11), (0, 3, 5, 0), (0, 0, 8, 4), (0, 0, 9, 7), (0, 0, 10, 0), (0, 3, 1, 11), (0, 3, 10, 11), (0, 3, 8, 6), (0, 3, 7, 6), (0, 2, 5, 0), (0, 0, 12, 4), (0, 2, 8, 4), (0, 2, 9, 7), (0, 2, 12, 7), (0, 0, 1, 2), (0, 0, 5, 0), (0, 1, 5, 6), (0, 2, 1, 11), (0, 1, 12, 7), (0, 3, 4, 8), (0, 3, 9, 7), (0, 3, 12, 8), (1, 3, 1), (0, 0, 14, 10), (0, 0, 15, 10), (0, 2, 14, 5), (0, 3, 15, 1), (1, 5, 3), (1, 5, 4), (1, 5, 1), (0, 0, 13, 12), (0, 2, 13, 12), (0, 1, 15, 1), (0, 2, 15, 10), (0, 3, 14, 10), (1, 4, 1), (0, 1, 14, 5), (1, 2, 0), (1, 2, 1), (1, 2, 2), (0, 1, 13, 12), (0, 3, 13, 12), (1, 3, 0), (1, 3, 2), (1, 6, 0), (1, 6, 1), (2, 3, 2, 3), (2, 2, 2, 3), (2, 1, 2, 3), (1, 6, 2), (1, 7, 6), (1, 6, 5), (2, 2, 12, 13), (2, 1, 13, 12), (2, 0, 13, 12), (2, 3, 13, 12), (1, 7, 2), (1, 7, 3), (2, 2, 13, 8), (2, 1, 12, 9), (2, 0, 12, 8), (2, 3, 12, 9), (2, 2, 7, 9), (2, 1, 7, 9), (1, 7, 7), (2, 0, 15, 1), (2, 0, 14, 5), (2, 2, 15, 10), (2, 3, 14, 10), (2, 3, 15, 1), (2, 1, 14, 10), (2, 1, 15, 10), (2, 2, 14, 5), (1, 4, 2), (1, 5, 2), (2, 2, 4, 8), (2, 0, 10, 11), (2, 3, 5, 0), (2, 1, 4, 8), (2, 1, 5, 0), (2, 0, 4, 8), (2, 3, 4, 8), (1, 4, 0), (2, 0, 0, 3), (2, 2, 1, 11), (2, 2, 8, 6), (2, 2, 9, 6), (2, 0, 1, 2), (2, 1, 8, 6), (2, 1, 9, 6), (2, 3, 10, 0), (2, 0, 9, 7), (2, 0, 5, 6), (2, 1, 1, 11), (2, 2, 10, 11), (2, 0, 8, 6), (2, 3, 9, 7), (2, 3, 8, 6), (2, 3, 1, 11), (2, 2, 5, 0), (2, 0, 7, 6), (2, 1, 10, 0), (2, 3, 7, 6), (2, 0, 11, 3), (2, 2, 6, 3), (2, 0, 2, 3), (2, 3, 0, 3), (2, 1, 11, 3), (2, 1, 6, 3), (2, 2, 11, 3), (2, 2, 0, 3), (2, 3, 11, 3), (2, 0, 6, 3), (2, 1, 0, 3), (2, 3, 6, 3))


N = len(HELD)
ROWS = 128
SENDS, TASKS, RETURNS = (tuple(s[1:] for s in STEPS if s[0] == kind) for kind in range(3))
OWN = ({i for _, _, i in SENDS} - {j for _, j, _ in SENDS}).pop()
PIECES = 1 + max(h for h, _, _ in SENDS)
PARTS = 1 + max(h for h, _, _ in RETURNS)


def parts(offset):
    return tuple((offset >> s) & 3 for s in (0, 2, 4)) + (offset >> 6,)


def minus(a, b):
    sizes = (4, 4, 4, 2)
    return tuple((p - q) % n for p, q, n in zip(parts(a), parts(b), sizes))


def weights():
    done, out = set(), []
    for g, h in TASKS:
        quad = [[0.0, 0.0], [0.0, 0.0]]
        for p in range(2):
            for q in range(2):
                a, b = HELD[2 * g + p], HELD[2 * h + q]
                there, back = minus(a, b), minus(b, a)
                if min(there, back) in done:
                    continue
                if g == h and p < q:
                    continue
                done.add(min(there, back))
                weight = 0.5 if there == back and any(there) else 1.0
                quad[p][q] = weight
                if g == h:
                    quad[q][p] = weight
        out.append(quad)
    assert len(done) == 72
    return out


def kernel(student_ref, teacher_ref, out_ref, held, pull, sent, come, g_send, g_recv, r_send, r_recv):
    gr, gc = lax.axis_index("gr"), lax.axis_index("gc")
    place = (lax.rem(gc // 2, 4), (gr // 4) * 2 + gc // 8, lax.rem(gr, 4), lax.rem(gc, 2))

    def device(step):
        x, y, z, c = (lax.rem(p + s, n) for p, s, n in zip(place, step, (4, 4, 4, 2)))
        return ((y // 2) * 4 + z, lax.rem(y, 2) * 8 + x * 2 + c)

    steps = set()
    for _, j, i in SENDS + RETURNS:
        steps |= {minus(HELD[i], HELD[j]), minus(HELD[j], HELD[i])}
    target = {step: device(step) for step in sorted(steps)}

    barrier = pltpu.get_barrier_semaphore()
    for step in target:
        pl.semaphore_signal(barrier, inc=1, device_id=target[step], device_id_type=MESH)

    def unit(ref, rows):
        values = ref[rows, :].astype(F32)
        inverse = lax.rsqrt(jnp.mean(values * values, axis=-1, keepdims=True) + 1e-06)
        return (values * inverse * D ** (-0.5)).astype(BF16), inverse

    def rows_of(h):
        return pl.ds(h * (ROWS // PIECES), ROWS // PIECES)

    def part_of(h):
        return pl.ds(h * (ROWS // PARTS), ROWS // PARTS)

    for h in range(PIECES):
        held[OWN, rows_of(h), 0:D] = unit(student_ref, rows_of(h))[0]
        held[OWN, rows_of(h), D : 2 * D] = unit(teacher_ref, rows_of(h))[0]
    pl.semaphore_wait(barrier, len(target))

    arrived = {(h, OWN) for h in range(PIECES)}
    gathers, returns = {}, {}

    def await_piece(h, j):
        if (h, j) not in arrived:
            gathers[h, j].wait_recv()
            arrived.add((h, j))

    weight_of = dict(zip(TASKS, weights()))
    fresh = set(range(N // 2))

    def add(g, value):
        value = value.reshape(2, ROWS, D)
        if g in fresh:
            pull[2 * g : 2 * g + 2] = value
            fresh.discard(g)
        else:
            pull[2 * g : 2 * g + 2] += value

    def dot(a, b, dims):
        return lax.dot_general(a, b, (dims, ((), ())), preferred_element_type=F32)

    def run(g, h):
        quad = weight_of[g, h]
        for b in (2 * g, 2 * g + 1, 2 * h, 2 * h + 1):
            for piece in range(PIECES):
                await_piece(piece, b)
        s_g = held[2 * g : 2 * g + 2, :, 0:D].reshape(2 * ROWS, D)
        s_h = held[2 * h : 2 * h + 2, :, 0:D].reshape(2 * ROWS, D)
        t_g = held[2 * g : 2 * g + 2, :, D : 2 * D].reshape(2 * ROWS, D)
        t_h = held[2 * h : 2 * h + 2, :, D : 2 * D].reshape(2 * ROWS, D)
        gap = dot(s_g, s_h, ((1,), (1,))) - dot(t_g, t_h, ((1,), (1,)))
        lines = []
        for p in range(2):
            line = []
            for q in range(2):
                if quad[p][q] == 0.0:
                    line.append(jnp.zeros((ROWS, ROWS), BF16))
                    continue
                part = gap[p * ROWS : (p + 1) * ROWS, q * ROWS : (q + 1) * ROWS]
                value = jnp.tanh(0.5 * D**0.5 * part).astype(BF16)
                line.append(value if quad[p][q] == 1.0 else value * jnp.asarray(quad[p][q], BF16))
            lines.append(jnp.concatenate(line, axis=1))
        mismatch = jnp.concatenate(lines, axis=0)
        add(g, dot(mismatch, s_h, ((1,), (0,))))
        if g != h:
            add(h, dot(mismatch, s_g, ((0,), (0,))))

    def send(h, j, i):
        await_piece(h, i)
        gathers[h, j] = pltpu.make_async_remote_copy(
            src_ref=held.at[i, rows_of(h), :],
            dst_ref=held.at[j, rows_of(h), :],
            send_sem=g_send.at[h, j],
            recv_sem=g_recv.at[h, j],
            device_id=target[minus(HELD[i], HELD[j])],
            device_id_type=MESH,
        )
        gathers[h, j].start()

    def total(h, j):
        value = pull[j, part_of(h), :]
        for part, child, goal in RETURNS:
            if (part, goal) == (h, j):
                returns[h, child].wait_recv()
                value += come[child, part_of(h), :].astype(F32)
        return value

    def give_back(h, j, i):
        sent[j, part_of(h), :] = total(h, j).astype(BF16)
        returns[h, j] = pltpu.make_async_remote_copy(
            src_ref=sent.at[j, part_of(h), :],
            dst_ref=come.at[j, part_of(h), :],
            send_sem=r_send.at[h, j],
            recv_sem=r_recv.at[h, j],
            device_id=target[minus(HELD[j], HELD[i])],
            device_id_type=MESH,
        )
        returns[h, j].start()

    for step in STEPS:
        (send, run, give_back)[step[0]](*step[1:])

    scale = 12.0 * (D / (ROWS * 128)) ** 0.5
    for h in range(PARTS):
        value = total(h, OWN)
        unit_float = held[OWN, part_of(h), 0:D].astype(F32)
        inverse = unit(student_ref, part_of(h))[1]
        radial = jnp.sum(unit_float * value, axis=-1, keepdims=True)
        out_ref[part_of(h), :] = scale * inverse * (value - radial * unit_float)
    for h, j, _ in SENDS:
        gathers[h, j].wait_send()
    for h, j, _ in RETURNS:
        returns[h, j].wait_send()


def local(student, teacher):
    vmem = pl.BlockSpec(memory_space=pltpu.VMEM)
    g_sems = pltpu.SemaphoreType.DMA((PIECES, N))
    r_sems = pltpu.SemaphoreType.DMA((PARTS, N))
    return pl.pallas_call(
        kernel,
        out_shape=jax.ShapeDtypeStruct((ROWS, D), F32),
        in_specs=[vmem, vmem],
        out_specs=vmem,
        scratch_shapes=[
            pltpu.VMEM((N, ROWS, 2 * D), BF16),
            pltpu.VMEM((N, ROWS, D), F32),
            pltpu.VMEM((N, ROWS, D), BF16),
            pltpu.VMEM((N, ROWS, D), BF16),
            g_sems,
            g_sems,
            r_sems,
            r_sems,
        ],
        compiler_params=pltpu.CompilerParams(
            collective_id=0, has_side_effects=True, vmem_limit_bytes=56 * 2**20
        ),
        name="relational_grad",
    )(student, teacher)


def solution(mesh):
    spec = P(("gr", "gc"), None)
    return jax.shard_map(local, mesh=mesh, in_specs=(spec, spec), out_specs=spec, check_vma=False)
```

```python
import jax
import jax.numpy as jnp
from jax import lax
from jax.experimental import pallas as pl
from jax.experimental.pallas import tpu as pltpu
from jax.sharding import PartitionSpec as P

D = 1024
F32 = jnp.float32
BF16 = jnp.bfloat16
MESH = pl.DeviceIdType.MESH

HELD = (112, 19, 67, 64, 69, 113, 1, 13, 5, 77, 32, 80, 9, 73, 33, 35)
STEPS = ((0, 0, 2, 3), (0, 1, 6, 3), (0, 1, 0, 3), (0, 3, 11, 3), (0, 0, 6, 3), (0, 0, 0, 3), (0, 1, 2, 3), (0, 1, 11, 3), (0, 2, 6, 3), (0, 2, 11, 3), (0, 3, 2, 3), (0, 3, 0, 3), (0, 1, 4, 6), (0, 1, 9, 6), (0, 0, 11, 3), (0, 2, 2, 3), (0, 2, 0, 3), (0, 3, 6, 3), (0, 0, 7, 6), (0, 0, 4, 6), (0, 1, 8, 4), (0, 1, 7, 9), (0, 1, 1, 11), (0, 1, 10, 0), (0, 2, 7, 6), (0, 2, 4, 6), (0, 2, 10, 11), (0, 3, 5, 0), (0, 0, 8, 4), (0, 0, 9, 7), (0, 0, 10, 0), (0, 3, 1, 11), (0, 3, 10, 11), (0, 3, 8, 6), (0, 3, 7, 6), (0, 2, 5, 0), (0, 0, 12, 4), (0, 2, 8, 4), (0, 2, 9, 7), (0, 2, 12, 7), (0, 0, 1, 2), (0, 0, 5, 0), (0, 1, 5, 6), (0, 2, 1, 11), (0, 1, 12, 7), (0, 3, 4, 8), (0, 3, 9, 7), (0, 3, 12, 8), (1, 3, 1), (0, 0, 14, 10), (0, 0, 15, 10), (0, 2, 14, 5), (0, 3, 15, 1), (1, 5, 3), (1, 5, 4), (1, 5, 1), (0, 0, 13, 12), (0, 2, 13, 12), (0, 1, 15, 1), (0, 2, 15, 10), (0, 3, 14, 10), (1, 4, 1), (0, 1, 14, 5), (1, 2, 0), (1, 2, 1), (1, 2, 2), (0, 1, 13, 12), (0, 3, 13, 12), (1, 3, 0), (1, 3, 2), (1, 6, 0), (1, 6, 1), (2, 3, 2, 3), (2, 2, 2, 3), (2, 1, 2, 3), (1, 6, 2), (1, 7, 6), (1, 6, 5), (2, 2, 12, 13), (2, 1, 13, 12), (2, 0, 13, 12), (2, 3, 13, 12), (1, 7, 2), (1, 7, 3), (2, 2, 13, 8), (2, 1, 12, 9), (2, 0, 12, 8), (2, 3, 12, 9), (2, 2, 7, 9), (2, 1, 7, 9), (1, 7, 7), (2, 0, 15, 1), (2, 0, 14, 5), (2, 2, 15, 10), (2, 3, 14, 10), (2, 3, 15, 1), (2, 1, 14, 10), (2, 1, 15, 10), (2, 2, 14, 5), (1, 4, 2), (1, 5, 2), (2, 2, 4, 8), (2, 0, 10, 11), (2, 3, 5, 0), (2, 1, 4, 8), (2, 1, 5, 0), (2, 0, 4, 8), (2, 3, 4, 8), (1, 4, 0), (2, 0, 0, 3), (2, 2, 1, 11), (2, 2, 8, 6), (2, 2, 9, 6), (2, 0, 1, 2), (2, 1, 8, 6), (2, 1, 9, 6), (2, 3, 10, 0), (2, 0, 9, 7), (2, 0, 5, 6), (2, 1, 1, 11), (2, 2, 10, 11), (2, 0, 8, 6), (2, 3, 9, 7), (2, 3, 8, 6), (2, 3, 1, 11), (2, 2, 5, 0), (2, 0, 7, 6), (2, 1, 10, 0), (2, 3, 7, 6), (2, 0, 11, 3), (2, 2, 6, 3), (2, 0, 2, 3), (2, 3, 0, 3), (2, 1, 11, 3), (2, 1, 6, 3), (2, 2, 11, 3), (2, 2, 0, 3), (2, 3, 11, 3), (2, 0, 6, 3), (2, 1, 0, 3), (2, 3, 6, 3))


N = len(HELD)
ROWS = 128
SENDS, TASKS, RETURNS = (tuple(s[1:] for s in STEPS if s[0] == kind) for kind in range(3))
OWN = ({i for _, _, i in SENDS} - {j for _, j, _ in SENDS}).pop()
PIECES = 1 + max(h for h, _, _ in SENDS)
PARTS = 1 + max(h for h, _, _ in RETURNS)


def parts(offset):
    return tuple((offset >> s) & 3 for s in (0, 2, 4)) + (offset >> 6,)


def minus(a, b):
    sizes = (4, 4, 4, 2)
    return tuple((p - q) % n for p, q, n in zip(parts(a), parts(b), sizes))


def weights():
    done, out = set(), []
    for g, h in TASKS:
        quad = [[0.0, 0.0], [0.0, 0.0]]
        for p in range(2):
            for q in range(2):
                a, b = HELD[2 * g + p], HELD[2 * h + q]
                there, back = minus(a, b), minus(b, a)
                if min(there, back) in done:
                    continue
                if g == h and p < q:
                    continue
                done.add(min(there, back))
                weight = 0.5 if there == back and any(there) else 1.0
                quad[p][q] = weight
                if g == h:
                    quad[q][p] = weight
        out.append(quad)
    assert len(done) == 72
    return out


def kernel(
    student_hbm, teacher_hbm, out_hbm, student_ref, teacher_ref, out_ref, held, pull, sent, come,
    in_sem, out_sem, g_send, g_recv, r_send, r_recv,
):
    gr, gc = lax.axis_index("gr"), lax.axis_index("gc")
    place = (lax.rem(gc // 2, 4), (gr // 4) * 2 + gc // 8, lax.rem(gr, 4), lax.rem(gc, 2))

    def device(step):
        x, y, z, c = (lax.rem(p + s, n) for p, s, n in zip(place, step, (4, 4, 4, 2)))
        return ((y // 2) * 4 + z, lax.rem(y, 2) * 8 + x * 2 + c)

    steps = set()
    for _, j, i in SENDS + RETURNS:
        steps |= {minus(HELD[i], HELD[j]), minus(HELD[j], HELD[i])}
    target = {step: device(step) for step in sorted(steps)}

    barrier = pltpu.get_barrier_semaphore()
    for step in target:
        pl.semaphore_signal(barrier, inc=1, device_id=target[step], device_id_type=MESH)

    loads = [
        pltpu.make_async_copy(student_hbm, student_ref, in_sem.at[0]),
        pltpu.make_async_copy(teacher_hbm, teacher_ref, in_sem.at[1]),
    ]
    for load in loads:
        load.start()
    for load in loads:
        load.wait()

    def unit(ref, rows):
        values = ref[rows, :].astype(F32)
        inverse = lax.rsqrt(jnp.mean(values * values, axis=-1, keepdims=True) + 1e-06)
        return (values * inverse * D ** (-0.5)).astype(BF16), inverse

    def rows_of(h):
        return pl.ds(h * (ROWS // PIECES), ROWS // PIECES)

    def part_of(h):
        return pl.ds(h * (ROWS // PARTS), ROWS // PARTS)

    for h in range(PIECES):
        held[OWN, rows_of(h), 0:D] = unit(student_ref, rows_of(h))[0]
        held[OWN, rows_of(h), D : 2 * D] = unit(teacher_ref, rows_of(h))[0]
    pl.semaphore_wait(barrier, len(target))

    arrived = {(h, OWN) for h in range(PIECES)}
    gathers, returns = {}, {}

    def await_piece(h, j):
        if (h, j) not in arrived:
            gathers[h, j].wait_recv()
            arrived.add((h, j))

    weight_of = dict(zip(TASKS, weights()))
    fresh = set(range(N // 2))

    def add(g, value):
        value = value.reshape(2, ROWS, D)
        if g in fresh:
            pull[2 * g : 2 * g + 2] = value
            fresh.discard(g)
        else:
            pull[2 * g : 2 * g + 2] += value

    def dot(a, b, dims):
        return lax.dot_general(a, b, (dims, ((), ())), preferred_element_type=F32)

    def run(g, h):
        quad = weight_of[g, h]
        for b in (2 * g, 2 * g + 1, 2 * h, 2 * h + 1):
            for piece in range(PIECES):
                await_piece(piece, b)
        s_g = held[2 * g : 2 * g + 2, :, 0:D].reshape(2 * ROWS, D)
        s_h = held[2 * h : 2 * h + 2, :, 0:D].reshape(2 * ROWS, D)
        t_g = held[2 * g : 2 * g + 2, :, D : 2 * D].reshape(2 * ROWS, D)
        t_h = held[2 * h : 2 * h + 2, :, D : 2 * D].reshape(2 * ROWS, D)
        gap = dot(s_g, s_h, ((1,), (1,))) - dot(t_g, t_h, ((1,), (1,)))
        lines = []
        for p in range(2):
            line = []
            for q in range(2):
                if quad[p][q] == 0.0:
                    line.append(jnp.zeros((ROWS, ROWS), BF16))
                    continue
                part = gap[p * ROWS : (p + 1) * ROWS, q * ROWS : (q + 1) * ROWS]
                value = jnp.tanh(0.5 * D**0.5 * part).astype(BF16)
                line.append(value if quad[p][q] == 1.0 else value * jnp.asarray(quad[p][q], BF16))
            lines.append(jnp.concatenate(line, axis=1))
        mismatch = jnp.concatenate(lines, axis=0)
        add(g, dot(mismatch, s_h, ((1,), (0,))))
        if g != h:
            add(h, dot(mismatch, s_g, ((0,), (0,))))

    def send(h, j, i):
        await_piece(h, i)
        gathers[h, j] = pltpu.make_async_remote_copy(
            src_ref=held.at[i, rows_of(h), :],
            dst_ref=held.at[j, rows_of(h), :],
            send_sem=g_send.at[h, j],
            recv_sem=g_recv.at[h, j],
            device_id=target[minus(HELD[i], HELD[j])],
            device_id_type=MESH,
        )
        gathers[h, j].start()

    def total(h, j):
        value = pull[j, part_of(h), :]
        for part, child, goal in RETURNS:
            if (part, goal) == (h, j):
                returns[h, child].wait_recv()
                value += come[child, part_of(h), :].astype(F32)
        return value

    def give_back(h, j, i):
        sent[j, part_of(h), :] = total(h, j).astype(BF16)
        returns[h, j] = pltpu.make_async_remote_copy(
            src_ref=sent.at[j, part_of(h), :],
            dst_ref=come.at[j, part_of(h), :],
            send_sem=r_send.at[h, j],
            recv_sem=r_recv.at[h, j],
            device_id=target[minus(HELD[j], HELD[i])],
            device_id_type=MESH,
        )
        returns[h, j].start()

    for step in STEPS:
        (send, run, give_back)[step[0]](*step[1:])

    stores = []
    scale = 12.0 * (D / (ROWS * 128)) ** 0.5
    for h in range(PARTS):
        value = total(h, OWN)
        unit_float = held[OWN, part_of(h), 0:D].astype(F32)
        inverse = unit(student_ref, part_of(h))[1]
        radial = jnp.sum(unit_float * value, axis=-1, keepdims=True)
        out_ref[part_of(h), :] = scale * inverse * (value - radial * unit_float)
        stores.append(
            pltpu.make_async_copy(out_ref.at[part_of(h), :], out_hbm.at[part_of(h), :], out_sem.at[h])
        )
        stores[-1].start()
    for h, j, _ in SENDS:
        gathers[h, j].wait_send()
    for h, j, _ in RETURNS:
        returns[h, j].wait_send()
    for store in stores:
        store.wait()


def local(student, teacher):
    hbm = pl.BlockSpec(memory_space=pl.ANY)
    g_sems = pltpu.SemaphoreType.DMA((PIECES, N))
    r_sems = pltpu.SemaphoreType.DMA((PARTS, N))
    return pl.pallas_call(
        kernel,
        out_shape=jax.ShapeDtypeStruct((ROWS, D), F32),
        in_specs=[hbm, hbm],
        out_specs=hbm,
        scratch_shapes=[
            pltpu.VMEM((ROWS, D), BF16),
            pltpu.VMEM((ROWS, D), BF16),
            pltpu.VMEM((ROWS, D), F32),
            pltpu.VMEM((N, ROWS, 2 * D), BF16),
            pltpu.VMEM((N, ROWS, D), F32),
            pltpu.VMEM((N, ROWS, D), BF16),
            pltpu.VMEM((N, ROWS, D), BF16),
            pltpu.SemaphoreType.DMA((2,)),
            pltpu.SemaphoreType.DMA((PARTS,)),
            g_sems,
            g_sems,
            r_sems,
            r_sems,
        ],
        compiler_params=pltpu.CompilerParams(
            collective_id=0, has_side_effects=True, vmem_limit_bytes=56 * 2**20
        ),
        name="relational_grad",
    )(student, teacher)


def solution(mesh):
    spec = P(("gr", "gc"), None)
    return jax.shard_map(local, mesh=mesh, in_specs=(spec, spec), out_specs=spec, check_vma=False)
```

```python
import jax
import jax.numpy as jnp
from jax import lax
from jax.experimental import pallas as pl
from jax.experimental.pallas import tpu as pltpu
from jax.sharding import PartitionSpec as P

D = 1024
F32 = jnp.float32
BF16 = jnp.bfloat16
MESH = pl.DeviceIdType.MESH

HELD = (1, 3, 73, 9, 33, 99, 0, 49, 5, 69, 83, 32, 13, 77, 112, 16)
STEPS = ((0, 0, 14, 6), (0, 2, 0, 6), (0, 2, 15, 6), (0, 3, 1, 6), (0, 1, 0, 6), (0, 2, 1, 6), (0, 2, 14, 6), (0, 3, 15, 6), (0, 0, 0, 6), (0, 0, 1, 6), (0, 0, 15, 6), (0, 1, 14, 6), (0, 2, 8, 0), (0, 2, 13, 0), (0, 1, 1, 6), (0, 1, 15, 6), (0, 3, 0, 6), (0, 3, 14, 6), (0, 1, 12, 0), (0, 1, 9, 0), (0, 2, 12, 13), (0, 2, 9, 8), (0, 0, 7, 14), (0, 2, 11, 14), (0, 3, 11, 15), (0, 3, 10, 15), (0, 0, 12, 0), (0, 0, 9, 0), (0, 1, 8, 9), (0, 1, 13, 12), (0, 0, 11, 14), (0, 2, 7, 14), (0, 3, 9, 0), (0, 3, 13, 0), (0, 1, 11, 15), (0, 1, 10, 15), (1, 7, 0), (1, 0, 0), (0, 1, 2, 12), (0, 2, 2, 9), (0, 0, 8, 9), (0, 0, 13, 12), (0, 0, 10, 1), (0, 1, 7, 0), (0, 2, 10, 15), (0, 3, 7, 14), (0, 0, 3, 8), (0, 3, 8, 9), (0, 3, 12, 13), (0, 3, 3, 13), (0, 3, 4, 11), (0, 3, 5, 10), (0, 1, 5, 11), (0, 2, 4, 7), (1, 7, 4), (1, 7, 6), (1, 6, 0), (0, 1, 3, 2), (0, 2, 3, 2), (0, 0, 4, 7), (0, 1, 4, 11), (0, 2, 5, 11), (1, 6, 6), (0, 0, 5, 10), (1, 7, 5), (1, 4, 3), (1, 5, 4), (0, 0, 2, 3), (0, 3, 2, 3), (2, 3, 9, 8), (2, 1, 9, 8), (2, 2, 8, 9), (2, 0, 9, 8), (1, 6, 3), (1, 1, 0), (2, 1, 8, 0), (2, 0, 8, 0), (1, 3, 1), (1, 5, 1), (1, 2, 1), (1, 7, 1), (2, 3, 3, 2), (2, 1, 2, 3), (2, 2, 14, 6), (2, 0, 2, 3), (2, 2, 3, 2), (2, 0, 15, 6), (2, 3, 15, 6), (1, 2, 0), (2, 3, 2, 8), (2, 1, 3, 13), (2, 0, 3, 13), (2, 2, 2, 9), (1, 2, 2), (1, 3, 2), (1, 6, 2), (2, 3, 5, 10), (2, 1, 4, 11), (2, 1, 5, 11), (2, 0, 4, 11), (2, 2, 5, 11), (2, 3, 4, 7), (2, 0, 5, 11), (2, 2, 4, 11), (1, 6, 5), (2, 3, 12, 13), (2, 3, 11, 14), (2, 3, 8, 0), (2, 1, 12, 13), (2, 2, 13, 12), (2, 0, 10, 1), (2, 1, 10, 15), (2, 2, 10, 15), (1, 3, 0), (2, 3, 13, 0), (2, 1, 7, 14), (2, 2, 1, 6), (2, 2, 7, 0), (2, 1, 13, 0), (2, 0, 7, 0), (2, 2, 12, 0), (2, 2, 9, 0), (2, 3, 10, 1), (2, 0, 13, 12), (2, 1, 11, 15), (2, 1, 1, 6), (2, 3, 7, 14), (2, 0, 12, 0), (2, 0, 1, 6), (2, 2, 11, 15), (2, 0, 11, 14), (2, 3, 0, 6), (2, 3, 1, 6), (2, 1, 0, 6), (2, 1, 14, 6), (2, 1, 15, 6), (2, 2, 0, 6), (2, 3, 14, 6), (2, 2, 15, 6), (2, 0, 14, 6), (2, 0, 0, 6))


N = len(HELD)
ROWS = 128
SENDS, TASKS, RETURNS = (tuple(s[1:] for s in STEPS if s[0] == kind) for kind in range(3))
OWN = ({i for _, _, i in SENDS} - {j for _, j, _ in SENDS}).pop()
PIECES = 1 + max(h for h, _, _ in SENDS)
PARTS = 1 + max(h for h, _, _ in RETURNS)


def parts(offset):
    return tuple((offset >> s) & 3 for s in (0, 2, 4)) + (offset >> 6,)


def minus(a, b):
    sizes = (4, 4, 4, 2)
    return tuple((p - q) % n for p, q, n in zip(parts(a), parts(b), sizes))


def weights():
    done, out = set(), []
    for g, h in TASKS:
        quad = [[0.0, 0.0], [0.0, 0.0]]
        for p in range(2):
            for q in range(2):
                a, b = HELD[2 * g + p], HELD[2 * h + q]
                there, back = minus(a, b), minus(b, a)
                if min(there, back) in done:
                    continue
                if g == h and p < q:
                    continue
                done.add(min(there, back))
                weight = 0.5 if there == back and any(there) else 1.0
                quad[p][q] = weight
                if g == h:
                    quad[q][p] = weight
        out.append(quad)
    assert len(done) == 72
    return out


def kernel(
    student_hbm, teacher_hbm, out_hbm, student_ref, teacher_ref, out_ref, inverse_ref, held, pull, sent, come,
    in_sem, out_sem, g_send, g_recv, r_send, r_recv,
):
    gr, gc = lax.axis_index("gr"), lax.axis_index("gc")
    place = (lax.rem(gc // 2, 4), (gr // 4) * 2 + gc // 8, lax.rem(gr, 4), lax.rem(gc, 2))

    def device(step):
        x, y, z, c = (lax.rem(p + s, n) for p, s, n in zip(place, step, (4, 4, 4, 2)))
        return ((y // 2) * 4 + z, lax.rem(y, 2) * 8 + x * 2 + c)

    steps = set()
    for _, j, i in SENDS + RETURNS:
        steps |= {minus(HELD[i], HELD[j]), minus(HELD[j], HELD[i])}
    target = {step: device(step) for step in sorted(steps)}

    barrier = pltpu.get_barrier_semaphore()
    for step in target:
        pl.semaphore_signal(barrier, inc=1, device_id=target[step], device_id_type=MESH)

    loads = [
        pltpu.make_async_copy(student_hbm, student_ref, in_sem.at[0]),
        pltpu.make_async_copy(teacher_hbm, teacher_ref, in_sem.at[1]),
    ]
    for load in loads:
        load.start()
    for load in loads:
        load.wait()

    def unit(ref, rows):
        values = ref[rows, :].astype(F32)
        inverse = lax.rsqrt(jnp.mean(values * values, axis=-1, keepdims=True) + 1e-06)
        return (values * inverse * D ** (-0.5)).astype(BF16), inverse

    def rows_of(h):
        return pl.ds(h * (ROWS // PIECES), ROWS // PIECES)

    def part_of(h):
        return pl.ds(h * (ROWS // PARTS), ROWS // PARTS)

    for h in range(PIECES):
        held[OWN, rows_of(h), 0:D], inverse = unit(student_ref, rows_of(h))
        inverse_ref[rows_of(h), :] = jnp.broadcast_to(inverse, (ROWS // PIECES, 128))
        held[OWN, rows_of(h), D : 2 * D] = unit(teacher_ref, rows_of(h))[0]
    pl.semaphore_wait(barrier, len(target))

    arrived = {(h, OWN) for h in range(PIECES)}
    gathers, returns = {}, {}

    def await_piece(h, j):
        if (h, j) not in arrived:
            gathers[h, j].wait_recv()
            arrived.add((h, j))

    weight_of = dict(zip(TASKS, weights()))
    fresh = set(range(N // 2))

    def add(g, value):
        value = value.reshape(2, ROWS, D)
        if g in fresh:
            pull[2 * g : 2 * g + 2] = value
            fresh.discard(g)
        else:
            pull[2 * g : 2 * g + 2] += value

    def dot(a, b, dims):
        return lax.dot_general(a, b, (dims, ((), ())), preferred_element_type=F32)

    def run(g, h):
        quad = weight_of[g, h]
        for b in (2 * g, 2 * g + 1, 2 * h, 2 * h + 1):
            for piece in range(PIECES):
                await_piece(piece, b)
        s_g = held[2 * g : 2 * g + 2, :, 0:D].reshape(2 * ROWS, D)
        s_h = held[2 * h : 2 * h + 2, :, 0:D].reshape(2 * ROWS, D)
        t_g = held[2 * g : 2 * g + 2, :, D : 2 * D].reshape(2 * ROWS, D)
        t_h = held[2 * h : 2 * h + 2, :, D : 2 * D].reshape(2 * ROWS, D)
        gap = dot(s_g, s_h, ((1,), (1,))) - dot(t_g, t_h, ((1,), (1,)))
        lines = []
        for p in range(2):
            line = []
            for q in range(2):
                if quad[p][q] == 0.0:
                    line.append(jnp.zeros((ROWS, ROWS), BF16))
                    continue
                part = gap[p * ROWS : (p + 1) * ROWS, q * ROWS : (q + 1) * ROWS]
                value = jnp.tanh(0.5 * D**0.5 * part).astype(BF16)
                line.append(value if quad[p][q] == 1.0 else value * jnp.asarray(quad[p][q], BF16))
            lines.append(jnp.concatenate(line, axis=1))
        mismatch = jnp.concatenate(lines, axis=0)
        add(g, dot(mismatch, s_h, ((1,), (0,))))
        if g != h:
            add(h, dot(mismatch, s_g, ((0,), (0,))))

    def send(h, j, i):
        await_piece(h, i)
        gathers[h, j] = pltpu.make_async_remote_copy(
            src_ref=held.at[i, rows_of(h), :],
            dst_ref=held.at[j, rows_of(h), :],
            send_sem=g_send.at[h, j],
            recv_sem=g_recv.at[h, j],
            device_id=target[minus(HELD[i], HELD[j])],
            device_id_type=MESH,
        )
        gathers[h, j].start()

    def total(h, j):
        value = pull[j, part_of(h), :]
        for part, child, goal in RETURNS:
            if (part, goal) == (h, j):
                returns[h, child].wait_recv()
                value += come[child, part_of(h), :].astype(F32)
        return value

    def give_back(h, j, i):
        sent[j, part_of(h), :] = total(h, j).astype(BF16)
        returns[h, j] = pltpu.make_async_remote_copy(
            src_ref=sent.at[j, part_of(h), :],
            dst_ref=come.at[j, part_of(h), :],
            send_sem=r_send.at[h, j],
            recv_sem=r_recv.at[h, j],
            device_id=target[minus(HELD[j], HELD[i])],
            device_id_type=MESH,
        )
        returns[h, j].start()

    last_task = max(n for n, step in enumerate(STEPS) if step[0] == 1)
    for n, step in enumerate(STEPS):
        (send, run, give_back)[step[0]](*step[1:])
        if n == last_task:
            for h, j, _ in SENDS:
                gathers[h, j].wait_send()

    for h, j, _ in RETURNS[:-N]:
        returns[h, j].wait_send()
    stores = []
    scale = 12.0 * (D / (ROWS * 128)) ** 0.5
    final = {h: n for n, (h, _, i) in enumerate(RETURNS) if i == OWN}
    for h in sorted(final, key=final.get):
        value = total(h, OWN)
        unit_float = held[OWN, part_of(h), 0:D].astype(F32)
        inverse = inverse_ref[part_of(h), 0:1]
        radial = jnp.sum(unit_float * value, axis=-1, keepdims=True)
        out_ref[part_of(h), :] = scale * inverse * (value - radial * unit_float)
        stores.append(
            pltpu.make_async_copy(out_ref.at[part_of(h), :], out_hbm.at[part_of(h), :], out_sem.at[h])
        )
        stores[-1].start()
    for h, j, _ in RETURNS[-N:]:
        returns[h, j].wait_send()
    for store in stores:
        store.wait()


def local(student, teacher):
    hbm = pl.BlockSpec(memory_space=pl.ANY)
    g_sems = pltpu.SemaphoreType.DMA((PIECES, N))
    r_sems = pltpu.SemaphoreType.DMA((PARTS, N))
    return pl.pallas_call(
        kernel,
        out_shape=jax.ShapeDtypeStruct((ROWS, D), F32),
        in_specs=[hbm, hbm],
        out_specs=hbm,
        scratch_shapes=[
            pltpu.VMEM((ROWS, D), BF16),
            pltpu.VMEM((ROWS, D), BF16),
            pltpu.VMEM((ROWS, D), F32),
            pltpu.VMEM((ROWS, 128), F32),
            pltpu.VMEM((N, ROWS, 2 * D), BF16),
            pltpu.VMEM((N, ROWS, D), F32),
            pltpu.VMEM((N, ROWS, D), BF16),
            pltpu.VMEM((N, ROWS, D), BF16),
            pltpu.SemaphoreType.DMA((2,)),
            pltpu.SemaphoreType.DMA((PARTS,)),
            g_sems,
            g_sems,
            r_sems,
            r_sems,
        ],
        compiler_params=pltpu.CompilerParams(
            collective_id=0, has_side_effects=True, vmem_limit_bytes=56 * 2**20
        ),
        name="relational_grad",
    )(student, teacher)


def solution(mesh):
    spec = P(("gr", "gc"), None)
    return jax.shard_map(local, mesh=mesh, in_specs=(spec, spec), out_specs=spec, check_vma=False)
```

```python
import jax
import jax.numpy as jnp
from jax import lax
from jax.experimental import pallas as pl
from jax.experimental.pallas import tpu as pltpu
from jax.sharding import PartitionSpec as P

D = 1024
F32 = jnp.float32
BF16 = jnp.bfloat16
MESH = pl.DeviceIdType.MESH

HELD = (1, 3, 73, 9, 33, 99, 0, 49, 5, 69, 83, 32, 13, 77, 112, 16)
STEPS = ((0, 0, 14, 6), (0, 2, 0, 6), (0, 2, 15, 6), (0, 3, 1, 6), (0, 1, 0, 6), (0, 2, 1, 6), (0, 2, 14, 6), (0, 3, 15, 6), (0, 0, 0, 6), (0, 0, 1, 6), (0, 0, 15, 6), (0, 1, 14, 6), (0, 2, 8, 0), (0, 2, 13, 0), (0, 1, 1, 6), (0, 1, 15, 6), (0, 3, 0, 6), (0, 3, 14, 6), (0, 1, 12, 0), (0, 1, 9, 0), (0, 2, 12, 13), (0, 2, 9, 8), (0, 0, 7, 14), (0, 2, 11, 14), (0, 3, 11, 15), (0, 3, 10, 15), (0, 0, 12, 0), (0, 0, 9, 0), (0, 1, 8, 9), (0, 1, 13, 12), (0, 0, 11, 14), (0, 2, 7, 14), (0, 3, 9, 0), (0, 3, 13, 0), (0, 1, 11, 15), (0, 1, 10, 15), (1, 7, 0), (1, 0, 0), (0, 1, 2, 12), (0, 2, 2, 9), (0, 0, 8, 9), (0, 0, 13, 12), (0, 0, 10, 1), (0, 1, 7, 0), (0, 2, 10, 15), (0, 3, 7, 14), (0, 0, 3, 8), (0, 3, 8, 9), (0, 3, 12, 13), (0, 3, 3, 13), (0, 3, 4, 11), (0, 3, 5, 10), (0, 1, 5, 11), (0, 2, 4, 7), (1, 7, 4), (1, 7, 6), (1, 6, 0), (0, 1, 3, 2), (0, 2, 3, 2), (0, 0, 4, 7), (0, 1, 4, 11), (0, 2, 5, 11), (1, 6, 6), (0, 0, 5, 10), (1, 7, 5), (1, 4, 3), (1, 5, 4), (0, 0, 2, 3), (0, 3, 2, 3), (2, 3, 9, 8), (2, 1, 9, 8), (2, 2, 8, 9), (2, 0, 9, 8), (1, 6, 3), (1, 1, 0), (2, 1, 8, 0), (2, 0, 8, 0), (1, 3, 1), (1, 5, 1), (1, 2, 1), (1, 7, 1), (2, 3, 3, 2), (2, 1, 2, 3), (2, 2, 14, 6), (2, 0, 2, 3), (2, 2, 3, 2), (2, 0, 15, 6), (2, 3, 15, 6), (1, 2, 0), (2, 3, 2, 8), (2, 1, 3, 13), (2, 0, 3, 13), (2, 2, 2, 9), (1, 2, 2), (1, 3, 2), (1, 6, 2), (2, 3, 5, 10), (2, 1, 4, 11), (2, 1, 5, 11), (2, 0, 4, 11), (2, 2, 5, 11), (2, 3, 4, 7), (2, 0, 5, 11), (2, 2, 4, 11), (1, 6, 5), (2, 3, 12, 13), (2, 3, 11, 14), (2, 3, 8, 0), (2, 1, 12, 13), (2, 2, 13, 12), (2, 0, 10, 1), (2, 1, 10, 15), (2, 2, 10, 15), (1, 3, 0), (2, 3, 13, 0), (2, 1, 7, 14), (2, 2, 1, 6), (2, 2, 7, 0), (2, 1, 13, 0), (2, 0, 7, 0), (2, 2, 12, 0), (2, 2, 9, 0), (2, 3, 10, 1), (2, 0, 13, 12), (2, 1, 11, 15), (2, 1, 1, 6), (2, 3, 7, 14), (2, 0, 12, 0), (2, 0, 1, 6), (2, 2, 11, 15), (2, 0, 11, 14), (2, 3, 0, 6), (2, 3, 1, 6), (2, 1, 0, 6), (2, 1, 14, 6), (2, 1, 15, 6), (2, 2, 0, 6), (2, 3, 14, 6), (2, 2, 15, 6), (2, 0, 14, 6), (2, 0, 0, 6))


N = len(HELD)
ROWS = 128
SENDS, TASKS, RETURNS = (tuple(s[1:] for s in STEPS if s[0] == kind) for kind in range(3))
OWN = ({i for _, _, i in SENDS} - {j for _, j, _ in SENDS}).pop()
PIECES = 1 + max(h for h, _, _ in SENDS)
PARTS = 1 + max(h for h, _, _ in RETURNS)


def parts(offset):
    return tuple((offset >> s) & 3 for s in (0, 2, 4)) + (offset >> 6,)


def minus(a, b):
    sizes = (4, 4, 4, 2)
    return tuple((p - q) % n for p, q, n in zip(parts(a), parts(b), sizes))


def weights():
    done, out = set(), []
    for g, h in TASKS:
        quad = [[0.0, 0.0], [0.0, 0.0]]
        for p in range(2):
            for q in range(2):
                a, b = HELD[2 * g + p], HELD[2 * h + q]
                there, back = minus(a, b), minus(b, a)
                if min(there, back) in done:
                    continue
                if g == h and p < q:
                    continue
                done.add(min(there, back))
                weight = 0.5 if there == back and any(there) else 1.0
                quad[p][q] = weight
                if g == h:
                    quad[q][p] = weight
        out.append(quad)
    assert len(done) == 72
    return out


def kernel(
    student_hbm, teacher_hbm, out_hbm, student_ref, teacher_ref, out_ref, inverse_ref, held, pull, sent, come,
    in_sem, out_sem, g_send, g_recv, r_send, r_recv,
):
    gr, gc = lax.axis_index("gr"), lax.axis_index("gc")
    place = (lax.rem(gc // 2, 4), (gr // 4) * 2 + gc // 8, lax.rem(gr, 4), lax.rem(gc, 2))

    def device(step):
        x, y, z, c = (lax.rem(p + s, n) for p, s, n in zip(place, step, (4, 4, 4, 2)))
        return ((y // 2) * 4 + z, lax.rem(y, 2) * 8 + x * 2 + c)

    steps = set()
    for _, j, i in SENDS + RETURNS:
        steps |= {minus(HELD[i], HELD[j]), minus(HELD[j], HELD[i])}
    target = {step: device(step) for step in sorted(steps)}

    barrier = pltpu.get_barrier_semaphore()
    for step in target:
        pl.semaphore_signal(barrier, inc=1, device_id=target[step], device_id_type=MESH)

    loads = [
        pltpu.make_async_copy(student_hbm, student_ref, in_sem.at[0]),
        pltpu.make_async_copy(teacher_hbm, teacher_ref, in_sem.at[1]),
    ]
    for load in loads:
        load.start()
    for load in loads:
        load.wait()

    def unit(ref, rows):
        values = ref[rows, :].astype(F32)
        inverse = lax.rsqrt(jnp.mean(values * values, axis=-1, keepdims=True) + 1e-06)
        return (values * inverse * D ** (-0.5)).astype(BF16), inverse

    def rows_of(h):
        return pl.ds(h * (ROWS // PIECES), ROWS // PIECES)

    def part_of(h):
        return pl.ds(h * (ROWS // PARTS), ROWS // PARTS)

    for h in range(PIECES):
        held[OWN, rows_of(h), 0:D], inverse = unit(student_ref, rows_of(h))
        inverse_ref[rows_of(h), :] = jnp.broadcast_to(inverse, (ROWS // PIECES, 128))
        held[OWN, rows_of(h), D : 2 * D] = unit(teacher_ref, rows_of(h))[0]
    pl.semaphore_wait(barrier, len(target))

    arrived = {(h, OWN) for h in range(PIECES)}
    gathers, returns = {}, {}

    def await_piece(h, j):
        if (h, j) not in arrived:
            gathers[h, j].wait_recv()
            arrived.add((h, j))

    weight_of = dict(zip(TASKS, weights()))
    fresh = set(range(N // 2))

    def add(g, value):
        value = value.reshape(2, ROWS, D)
        if g in fresh:
            pull[2 * g : 2 * g + 2] = value
            fresh.discard(g)
        else:
            pull[2 * g : 2 * g + 2] += value

    def dot(a, b, dims):
        return lax.dot_general(a, b, (dims, ((), ())), preferred_element_type=F32)

    def run(g, h):
        quad = weight_of[g, h]
        for b in (2 * g, 2 * g + 1, 2 * h, 2 * h + 1):
            for piece in range(PIECES):
                await_piece(piece, b)
        s_g = held[2 * g : 2 * g + 2, :, 0:D].reshape(2 * ROWS, D)
        s_h = held[2 * h : 2 * h + 2, :, 0:D].reshape(2 * ROWS, D)
        t_g = held[2 * g : 2 * g + 2, :, D : 2 * D].reshape(2 * ROWS, D)
        t_h = held[2 * h : 2 * h + 2, :, D : 2 * D].reshape(2 * ROWS, D)
        gap = dot(s_g, s_h, ((1,), (1,))) - dot(t_g, t_h, ((1,), (1,)))
        lines = []
        for p in range(2):
            line = []
            for q in range(2):
                if quad[p][q] == 0.0:
                    line.append(jnp.zeros((ROWS, ROWS), BF16))
                    continue
                part = gap[p * ROWS : (p + 1) * ROWS, q * ROWS : (q + 1) * ROWS]
                value = jnp.tanh(0.5 * D**0.5 * part).astype(BF16)
                line.append(value if quad[p][q] == 1.0 else value * jnp.asarray(quad[p][q], BF16))
            lines.append(jnp.concatenate(line, axis=1))
        mismatch = jnp.concatenate(lines, axis=0)
        add(g, dot(mismatch, s_h, ((1,), (0,))))
        if g != h:
            add(h, dot(mismatch, s_g, ((0,), (0,))))

    def send(h, j, i):
        await_piece(h, i)
        gathers[h, j] = pltpu.make_async_remote_copy(
            src_ref=held.at[i, rows_of(h), :],
            dst_ref=held.at[j, rows_of(h), :],
            send_sem=g_send.at[h, j],
            recv_sem=g_recv.at[h, j],
            device_id=target[minus(HELD[i], HELD[j])],
            device_id_type=MESH,
        )
        gathers[h, j].start()

    def total(h, j):
        value = pull[j, part_of(h), :]
        for part, child, goal in RETURNS:
            if (part, goal) == (h, j):
                returns[h, child].wait_recv()
                value += come[child, part_of(h), :].astype(F32)
        return value

    def give_back(h, j, i):
        sent[j, part_of(h), :] = total(h, j).astype(BF16)
        returns[h, j] = pltpu.make_async_remote_copy(
            src_ref=sent.at[j, part_of(h), :],
            dst_ref=come.at[j, part_of(h), :],
            send_sem=r_send.at[h, j],
            recv_sem=r_recv.at[h, j],
            device_id=target[minus(HELD[j], HELD[i])],
            device_id_type=MESH,
        )
        returns[h, j].start()

    last_task = max(n for n, step in enumerate(STEPS) if step[0] == 1)
    for n, step in enumerate(STEPS):
        (send, run, give_back)[step[0]](*step[1:])
        if n == last_task:
            for h, j, _ in SENDS:
                gathers[h, j].wait_send()

    for h, j, _ in RETURNS[:-N]:
        returns[h, j].wait_send()
    stores = []
    scale = 12.0 * (D / (ROWS * 128)) ** 0.5
    final = {h: n for n, (h, _, i) in enumerate(RETURNS) if i == OWN}
    for h in sorted(final, key=final.get):
        value = total(h, OWN)
        unit_float = held[OWN, part_of(h), 0:D].astype(F32)
        inverse = inverse_ref[part_of(h), 0:1]
        radial = jnp.sum(unit_float * value, axis=-1, keepdims=True)
        out_ref[part_of(h), :] = scale * inverse * (value - radial * unit_float)
        stores.append(
            pltpu.make_async_copy(out_ref.at[part_of(h), :], out_hbm.at[part_of(h), :], out_sem.at[h])
        )
        stores[-1].start()
    for h, j, _ in RETURNS[-N:]:
        returns[h, j].wait_send()
    for store in stores:
        store.wait()


def hand_on(in_ref, out_ref):
    out_ref[...] = in_ref[...]


def local(student, teacher):
    hbm = pl.BlockSpec(memory_space=pl.ANY)
    g_sems = pltpu.SemaphoreType.DMA((PIECES, N))
    r_sems = pltpu.SemaphoreType.DMA((PARTS, N))
    result = pl.pallas_call(
        kernel,
        out_shape=jax.ShapeDtypeStruct((ROWS, D), F32),
        in_specs=[hbm, hbm],
        out_specs=hbm,
        scratch_shapes=[
            pltpu.VMEM((ROWS, D), BF16),
            pltpu.VMEM((ROWS, D), BF16),
            pltpu.VMEM((ROWS, D), F32),
            pltpu.VMEM((ROWS, 128), F32),
            pltpu.VMEM((N, ROWS, 2 * D), BF16),
            pltpu.VMEM((N, ROWS, D), F32),
            pltpu.VMEM((N, ROWS, D), BF16),
            pltpu.VMEM((N, ROWS, D), BF16),
            pltpu.SemaphoreType.DMA((2,)),
            pltpu.SemaphoreType.DMA((PARTS,)),
            g_sems,
            g_sems,
            r_sems,
            r_sems,
        ],
        compiler_params=pltpu.CompilerParams(
            collective_id=0, has_side_effects=True, vmem_limit_bytes=56 * 2**20
        ),
        name="relational_grad",
    )(student, teacher)
    vmem = pl.BlockSpec(memory_space=pltpu.VMEM)
    return pl.pallas_call(
        hand_on,
        out_shape=jax.ShapeDtypeStruct((ROWS, D), F32),
        in_specs=[vmem],
        out_specs=vmem,
        name="hand_on",
    )(result)


def solution(mesh):
    spec = P(("gr", "gc"), None)
    return jax.shard_map(local, mesh=mesh, in_specs=(spec, spec), out_specs=spec, check_vma=False)
```
